32 devices in a mesh: grp: 2 (over y), lat: 8 (over z, x), layer: 2 (over core).
Axes of the slice: x: 2, y: 2, z: 4, core: 2. Of those that a mesh axis runs over, the one named last changes fastest.
Arguments:
- resid: bfloat16 [2, 1024, 2048], P('layer', 'grp'), parts along dimension 1, may hold values from -6 to 6
- targets: bfloat16 [1024, 2, 2048], P(('grp', 'lat', 'layer')), parts along dimension 0, may hold values from -6 to 6
- encoder: bfloat16 [2, 16384, 2048], P('layer', 'lat'), may hold values from -0.125 to 0.125
- enc_bias: float32 [2, 16384], P('layer', 'lat'), may hold values from -4 to 4
- decoder: bfloat16 [2, 2, 16384, 2048], P('layer', None, 'lat'), may hold values from -0.09375 to 0.09375
- blocks: int32 [2, 8, 32], P('layer', 'grp'), parts along dimension 1, may hold values from 0 to 127, all different within a row
Outputs:
- grad_encoder: bfloat16 [4, 16384, 2048], P(('grp', 'layer'), 'lat'), parts along dimension 0
- grad_decoder: bfloat16 [4, 2, 16384, 2048], P(('grp', 'layer'), None, 'lat'), parts along dimension 0
- encoder_bias_gradient: float32 [4, 16384], P(('grp', 'layer'), 'lat'), parts along dimension 0
The draws below stay inside these ranges and needn't reach their ends.
There are 2 independent parts, one for each index of `grp`. The reference program is written for one: setup_inputs(seed, part) draws one part's arguments, and reference() takes and returns one part's arrays. A program takes and returns all parts, laid end to end along the dimension named above; an argument that names none is the same for every part. Nothing has to cross between parts.
Inputs may be any that keep to these rules, and one draw needn't show every extreme that they name: Each row of a tile lists 32 different blocks; every block is listed somewhere.
All inputs are finite; a program needn't handle non-finite values.
Results may differ from the reference program's by a relative error of at most 0.006.
Values may be sent and summed in bfloat16 or wider, within the bound.
A program may use at most 192 MiB of HBM per device.

```python
import math
import jax
import jax.numpy as jnp
from jax import lax

D = 2048
LATENTS = 16384
LAYERS = 2
BLOCK = 128
TILE = 128
ACTIVE = 32
TOKENS = 512
TILES = 4


def steps_of(stream_key, extent, pieces, least, high):
    def one(position, parts):
        heights = jax.random.uniform(jax.random.fold_in(jax.random.fold_in(stream_key, 6), position), (parts,), jnp.float32, least / len(pieces), high / len(pieces))
        return jnp.repeat(jnp.exp(heights), extent[position] // parts).reshape((-1,) + (1,) * (len(extent) - position - 1))

    loudness = one(*pieces[0])
    for cut in pieces[1:]:
        loudness = loudness * one(*cut)
    return loudness


def distinct(key, rows, count, top, lift):
    ranking = jax.random.permutation(jax.random.fold_in(key, 1), count)
    favour = ranking
    for power in range(3):
        favour = favour * favour // count
    favour = favour * lift // count
    tickets = jax.random.randint(jax.random.fold_in(key, 2), (rows, count), 0, 4096) + favour
    holders = jax.random.permutation(jax.random.fold_in(key, 3), rows)[jnp.arange(count) % rows]
    tickets = jnp.where(jnp.arange(rows)[:, None] == holders[None, :], 1 << 14, tickets)
    score = tickets * count + jnp.arange(count)
    return lax.top_k(score.astype(jnp.int32), top)[1].astype(jnp.int32)


def centred(rng, extent, scale, reach, cuts=(), held_as=jnp.bfloat16):
    result = jax.random.normal(rng, extent, jnp.float32) * scale
    if len(cuts) > 0:
        result = steps_of(rng, extent, cuts, -0.22, 0.18) * result
    return jnp.clip(result, min=-reach, max=reach).astype(held_as)


def setup_inputs(seed: int = 0, part: int = 0) -> dict:
    key_list = jax.random.split(jax.random.key(seed), 7)
    part_keys = jax.random.split(jax.random.fold_in(key_list[6], part), 7)
    resid = centred(part_keys[0], (LAYERS, TOKENS, D), 1.0, 6.0, ((0, 2),))
    targets = centred(part_keys[1], (TOKENS, LAYERS, D), 1.0, 6.0, ((0, 16),))
    encoder = centred(key_list[2], (LAYERS, LATENTS, D), D ** -0.5, 0.125, ((0, 2), (1, 8)))
    enc_bias = centred(key_list[3], (LAYERS, LATENTS), 1.0, 4.0, ((0, 2), (1, 8)), jnp.float32)
    decoder = centred(key_list[4], (LAYERS, LAYERS, LATENTS, D), (ACTIVE * BLOCK) ** -0.5, 0.09375, ((0, 2), (2, 8)))
    blocks = distinct(part_keys[5], LAYERS * TILES, LATENTS // BLOCK, ACTIVE, 4096).reshape((LAYERS, TILES, ACTIVE))
    return {"resid": resid, "targets": targets, "encoder": encoder, "enc_bias": enc_bias, "decoder": decoder, "blocks": blocks}


def tile_gate(enumerated_items, lat_block):
    hits = jnp.any(enumerated_items[:, :, None] == lat_block[None, None, :], axis=1).astype(jnp.float32)
    return jnp.repeat(hits, TILE, axis=0)

def reference(resid, targets, encoder, enc_bias, decoder, blocks):
    lat_block = (jnp.arange(LATENTS, dtype=jnp.int32) // BLOCK).astype(jnp.int32)
    gates = []
    acts = []
    for s in range(LAYERS):
        gate = tile_gate(blocks[s], lat_block)
        preactivation = jnp.dot(resid[s], encoder[s].T, preferred_element_type=jnp.float32) + enc_bias[s][None, :]
        gates.append(gate)
        acts.append((preactivation * gate).astype(jnp.bfloat16))
    recon = jnp.zeros((TOKENS, LAYERS, D), jnp.float32)
    for s in range(LAYERS):
        for t in range(LAYERS):
            recon = recon.at[:, t].add(jnp.dot(acts[s], decoder[s, t], preferred_element_type=jnp.float32))
    error_signal = ((recon - targets.astype(jnp.float32)) / math.sqrt(TOKENS)).astype(jnp.bfloat16)
    grad_dec = []
    grad_enc = []
    encoder_bias_gradient = []
    for s in range(LAYERS):
        gradient_per_row = []
        grad_act = jnp.zeros((TOKENS, LATENTS), jnp.float32)
        for t in range(LAYERS):
            gradient_per_row.append(jnp.dot(acts[s].T, error_signal[:, t], preferred_element_type=jnp.float32).astype(jnp.bfloat16))
            grad_act = grad_act + jnp.dot(error_signal[:, t], decoder[s, t].T, preferred_element_type=jnp.float32)
        grad_dec.append(jnp.stack(gradient_per_row))
        preactivation_gradient = grad_act * gates[s]
        encoder_bias_gradient.append(lax.optimization_barrier(jnp.sum(preactivation_gradient, axis=0)))
        grad_enc.append(jnp.dot(preactivation_gradient.astype(jnp.bfloat16).T, resid[s], preferred_element_type=jnp.float32).astype(jnp.bfloat16))
    return (jnp.stack(grad_enc), jnp.stack(grad_dec), jnp.stack(encoder_bias_gradient))
```

```python
import functools
import math

import jax
import jax.numpy as jnp
from jax import lax
from jax.experimental import pallas as pl
from jax.experimental.pallas import tpu as pltpu
from jax.sharding import PartitionSpec as P

BLOCK = 128
TILE = 128
CHUNKS = 4
MIB = 1 << 20
MESH = pl.DeviceIdType.MESH


def dot_nt(a, b):
    return lax.dot_general(a, b, (((1,), (1,)), ((), ())), preferred_element_type=jnp.float32)


def dot_nn(a, b):
    return jnp.dot(a, b, preferred_element_type=jnp.float32)


def chunk_place(k, width, cc):
    per = width // cc
    return k // per, (k % per) * cc


def decode_kernel(hits, resid_ref, enc_ref, bias_ref, dec_ref, act_ref, recon_ref, acc_ref):
    b = pl.program_id(0)
    chunks, tokens, cc = recon_ref.shape
    width = dec_ref.shape[2]

    @pl.when(b == 0)
    def _():
        acc_ref[...] = jnp.zeros_like(acc_ref)

    for n in range(tokens // TILE):
        rows = slice(n * TILE, (n + 1) * TILE)
        hit = hits[n, b]

        @pl.when(hit > 0)
        def _(rows=rows):
            a = (dot_nt(resid_ref[rows], enc_ref[...]) + bias_ref[...]).astype(jnp.bfloat16)
            act_ref[0, rows] = a
            for k in range(chunks):
                t, col = chunk_place(k, width, cc)
                acc_ref[k, rows] += dot_nn(a, dec_ref[t, :, col : col + cc])

        @pl.when(hit == 0)
        def _(rows=rows):
            act_ref[0, rows] = jnp.zeros((TILE, BLOCK), jnp.bfloat16)

    @pl.when(b == pl.num_programs(0) - 1)
    def _():
        recon_ref[...] = acc_ref[...].astype(jnp.bfloat16)


def encode_decode(hits, resid, encoder, enc_bias, decoder, chunks):
    tokens, width = resid.shape
    latents = encoder.shape[0]
    targets = decoder.shape[0]
    nb = latents // BLOCK
    cc = targets * width // chunks
    return pl.pallas_call(
        decode_kernel,
        grid_spec=pltpu.PrefetchScalarGridSpec(
            num_scalar_prefetch=1,
            grid=(nb,),
            in_specs=[
                pl.BlockSpec((tokens, width), lambda b, h: (0, 0)),
                pl.BlockSpec((BLOCK, width), lambda b, h: (b, 0)),
                pl.BlockSpec((1, BLOCK), lambda b, h: (0, b)),
                pl.BlockSpec((targets, BLOCK, width), lambda b, h: (0, b, 0)),
            ],
            out_specs=[
                pl.BlockSpec((1, tokens, BLOCK), lambda b, h: (b, 0, 0)),
                pl.BlockSpec((chunks, tokens, cc), lambda b, h: (0, 0, 0)),
            ],
            scratch_shapes=[pltpu.VMEM((chunks, tokens, cc), jnp.float32)],
        ),
        out_shape=[
            jax.ShapeDtypeStruct((nb, tokens, BLOCK), jnp.bfloat16),
            jax.ShapeDtypeStruct((chunks, tokens, cc), jnp.bfloat16),
        ],
        compiler_params=pltpu.CompilerParams(vmem_limit_bytes=48 * MIB),
        name="encode_decode",
    )(hits, resid, encoder, enc_bias, decoder)


def grads_kernel(hits, act_ref, dec_ref, sig_ref, resid_ref, genc_ref, gdec_ref, bias_ref):
    b = pl.program_id(0)
    chunks, tokens, cc = sig_ref.shape
    width = dec_ref.shape[2]
    tiles = tokens // TILE
    flags = [hits[n, b] for n in range(tiles)]
    count = sum(flags)
    first = jnp.int32(tiles - 1)
    for n in reversed(range(tiles)):
        first = jnp.where(flags[n] > 0, n, first)
    last = jnp.int32(0)
    for n in range(tiles):
        last = jnp.where(flags[n] > 0, n, last)

    def work(places, masks):
        rows = [pl.ds(pl.multiple_of(n * TILE, TILE), TILE) for n in places]
        back = []
        total = jnp.zeros((1, BLOCK), jnp.float32)
        for r, mask in zip(rows, masks):
            ga = jnp.zeros((TILE, BLOCK), jnp.float32)
            for k in range(chunks):
                t, col = chunk_place(k, width, cc)
                ga = ga + dot_nt(sig_ref[k, r], dec_ref[t, :, col : col + cc])
            if mask is not None:
                ga = ga * mask.astype(jnp.float32)
            total = total + jnp.sum(ga, axis=0, keepdims=True)
            back.append(ga.T.astype(jnp.bfloat16))
        bias_ref[...] = total
        acts = [act_ref[0, r].astype(jnp.float32).T.astype(jnp.bfloat16) for r in rows]
        for k in range(chunks):
            t, col = chunk_place(k, width, cc)
            out = dot_nn(acts[0], sig_ref[k, rows[0]])
            for i in range(1, len(rows)):
                out = out + dot_nn(acts[i], sig_ref[k, rows[i]])
            gdec_ref[t, :, col : col + cc] = out.astype(jnp.bfloat16)
        step = 1024 if width % 1024 == 0 else width
        for col in range(0, width, step):
            out = dot_nn(back[0], resid_ref[rows[0], col : col + step])
            for i in range(1, len(rows)):
                out = out + dot_nn(back[i], resid_ref[rows[i], col : col + step])
            genc_ref[:, col : col + step] = out.astype(jnp.bfloat16)

    @pl.when(count == 0)
    def _():
        bias_ref[...] = jnp.zeros_like(bias_ref)
        gdec_ref[...] = jnp.zeros_like(gdec_ref)
        genc_ref[...] = jnp.zeros_like(genc_ref)

    @pl.when(count == 1)
    def _():
        work([first], [None])

    @pl.when(count == 2)
    def _():
        work([first, last], [None, None])

    @pl.when(count > 2)
    def _():
        work(list(range(tiles)), flags)


def grads(hits, act, decoder, signal, resid):
    tokens, width = resid.shape
    targets, latents = decoder.shape[:2]
    chunks, _, cc = signal.shape
    nb = latents // BLOCK
    return pl.pallas_call(
        grads_kernel,
        grid_spec=pltpu.PrefetchScalarGridSpec(
            num_scalar_prefetch=1,
            grid=(nb,),
            in_specs=[
                pl.BlockSpec((1, tokens, BLOCK), lambda b, h: (b, 0, 0)),
                pl.BlockSpec((targets, BLOCK, width), lambda b, h: (0, b, 0)),
                pl.BlockSpec((chunks, tokens, cc), lambda b, h: (0, 0, 0)),
                pl.BlockSpec((tokens, width), lambda b, h: (0, 0)),
            ],
            out_specs=[
                pl.BlockSpec((BLOCK, width), lambda b, h: (b, 0)),
                pl.BlockSpec((targets, BLOCK, width), lambda b, h: (0, b, 0)),
                pl.BlockSpec((1, BLOCK), lambda b, h: (0, b)),
            ],
        ),
        out_shape=[
            jax.ShapeDtypeStruct((latents, width), jnp.bfloat16),
            jax.ShapeDtypeStruct((targets, latents, width), jnp.bfloat16),
            jax.ShapeDtypeStruct((1, latents), jnp.float32),
        ],
        compiler_params=pltpu.CompilerParams(vmem_limit_bytes=48 * MIB),
        name="gradients",
    )(hits, act, decoder, signal, resid)


def exchange_kernel(
    scale, p_ref, tgt_ref, out_ref, r0, s1, r1, s2, r2,
    core_send, core_recv, x_send, x_recv, z_send, z_recv,
):
    chunks, zs, xs, cores, rows, cc = p_ref.shape
    lat = lax.axis_index("lat")
    c = lax.axis_index("layer")
    z, x = lat // xs, lax.rem(lat, xs)
    f32 = jnp.float32

    def dev(dz, dx, dc):
        zz, xx = lax.rem(z + dz, zs), lax.rem(x + dx, xs)
        return {"lat": zz * xs + xx, "layer": lax.rem(c + dc, cores)}

    peers = [dev(0, 0, d) for d in range(1, cores)]
    peers += [dev(0, d, 0) for d in range(1, xs)]
    peers += [dev(d, 0, 0) for d in range(1, zs)]
    barrier = pltpu.get_barrier_semaphore()
    for peer in peers:
        pl.semaphore_signal(barrier, inc=1, device_id=peer, device_id_type=MESH)
    pl.semaphore_wait(barrier, len(peers))

    started = []

    def copy(src, dst, send, recv, to):
        return pltpu.make_async_remote_copy(
            src_ref=src, dst_ref=dst, send_sem=send, recv_sem=recv, device_id=to, device_id_type=MESH
        )

    def go(*a):
        d = copy(*a)
        d.start()
        started.append(d)

    def core_rs(k, d):
        to = lax.rem(c + d, cores)
        return (p_ref.at[k, :, :, to], r0.at[k, d - 1], core_send.at[0, k, d - 1],
                core_recv.at[0, k, d - 1], dev(0, 0, d))

    def x_rs(k, d):
        return (s1.at[k, d - 1], r1.at[k, d - 1], x_send.at[0, k, d - 1], x_recv.at[0, k, d - 1],
                dev(0, d, 0))

    def z_rs(k, d):
        return (s2.at[k, d - 1], r2.at[k, d - 1], z_send.at[0, k, d - 1], z_recv.at[0, k, d - 1],
                dev(d, 0, 0))

    def z_ag(k, d, zz):
        at = out_ref.at[k, zz, x, c]
        return (at, at, z_send.at[1, k, d - 1], z_recv.at[1, k, d - 1], dev(d, 0, 0))

    def x_ag(k, d, xx):
        at = out_ref.at[k, :, xx, c]
        return (at, at, x_send.at[1, k, d - 1], x_recv.at[1, k, d - 1], dev(0, d, 0))

    def core_ag(k, d, c2):
        at = out_ref.at[k, :, :, c2]
        return (at, at, core_send.at[1, k, d - 1], core_recv.at[1, k, d - 1], dev(0, 0, d))

    def part(k, zz, xx):
        total = p_ref[k, zz, xx, c].astype(f32)
        for i in range(cores - 1):
            total = total + r0[k, i, zz, xx].astype(f32)
        return total

    def stage_a(k):
        for d in range(1, cores):
            go(*core_rs(k, d))

    def stage_b(k):
        for d in range(1, cores):
            copy(*core_rs(k, d)).wait_recv()
        for d in range(1, xs):
            xx = lax.rem(x + d, xs)
            for zz in range(zs):
                s1[k, d - 1, zz] = part(k, zz, xx).astype(jnp.bfloat16)
            go(*x_rs(k, d))

    def line(k, zz):
        total = part(k, zz, x)
        for i in range(xs - 1):
            total = total + r1[k, i, zz].astype(f32)
        return total

    def stage_c(k):
        for d in range(1, xs):
            copy(*x_rs(k, d)).wait_recv()
        for d in range(1, zs):
            s2[k, d - 1] = line(k, lax.rem(z + d, zs)).astype(jnp.bfloat16)
            go(*z_rs(k, d))

    def stage_d(k):
        total = line(k, z)
        for d in range(1, zs):
            copy(*z_rs(k, d)).wait_recv()
            total = total + r2[k, d - 1].astype(f32)
        out_ref[k, z, x, c] = ((total - tgt_ref[k].astype(f32)) / scale).astype(jnp.bfloat16)
        for d in range(1, zs):
            go(*z_ag(k, d, z))

    def stage_e(k):
        for d in range(1, zs):
            copy(*z_ag(k, d, lax.rem(z - d + zs, zs))).wait_recv()
        for d in range(1, xs):
            go(*x_ag(k, d, x))

    def stage_f(k):
        for d in range(1, xs):
            copy(*x_ag(k, d, lax.rem(x - d + xs, xs))).wait_recv()
        for d in range(1, cores):
            go(*core_ag(k, d, c))

    def stage_g(k):
        for d in range(1, cores):
            copy(*core_ag(k, d, lax.rem(c - d + cores, cores))).wait_recv()

    stages = (stage_b, stage_c, stage_d, stage_e, stage_f, stage_g)
    for k in range(chunks):
        stage_a(k)
    for s in range(chunks + len(stages) - 1):
        for i, stage in enumerate(stages):
            if 0 <= s - i < chunks:
                stage(s - i)
    for d in started:
        d.wait_send()


def exchange(recon, targets, zs, xs, cores, scale):
    chunks, tokens, cc = recon.shape
    rows = tokens // (zs * xs * cores)
    bf16 = jnp.bfloat16
    dma = pltpu.SemaphoreType.DMA
    out = pl.pallas_call(
        functools.partial(exchange_kernel, scale),
        out_shape=jax.ShapeDtypeStruct((chunks, zs, xs, cores, rows, cc), bf16),
        in_specs=[pl.BlockSpec(memory_space=pltpu.VMEM)] * 2,
        out_specs=pl.BlockSpec(memory_space=pltpu.VMEM),
        scratch_shapes=[
            pltpu.VMEM((chunks, cores - 1, zs, xs, rows, cc), bf16),
            pltpu.VMEM((chunks, xs - 1, zs, rows, cc), bf16),
            pltpu.VMEM((chunks, xs - 1, zs, rows, cc), bf16),
            pltpu.VMEM((chunks, zs - 1, rows, cc), bf16),
            pltpu.VMEM((chunks, zs - 1, rows, cc), bf16),
            dma((2, chunks, cores - 1)),
            dma((2, chunks, cores - 1)),
            dma((2, chunks, xs - 1)),
            dma((2, chunks, xs - 1)),
            dma((2, chunks, zs - 1)),
            dma((2, chunks, zs - 1)),
        ],
        compiler_params=pltpu.CompilerParams(
            collective_id=0, has_side_effects=True, vmem_limit_bytes=40 * MIB
        ),
        name="exchange",
    )(recon.reshape(chunks, zs, xs, cores, rows, cc), targets)
    return out.reshape(chunks, tokens, cc)


def per_device(lat_size, layer_size, resid, targets, encoder, enc_bias, decoder, blocks):
    lat_count = encoder.shape[1]
    width = resid.shape[2]
    tokens = resid.shape[1]
    outs = decoder.shape[1]
    nb = lat_count // BLOCK
    lat_block = lax.axis_index("lat") * nb + jnp.arange(nb, dtype=jnp.int32)
    hits = jnp.any(blocks[0][:, :, None] == lat_block[None, None, :], axis=1).astype(jnp.int32)
    scale = math.sqrt(tokens)
    act, recon = encode_decode(hits, resid[0], encoder[0], enc_bias, decoder[0], CHUNKS)
    rows = targets.shape[0]
    cc = outs * width // CHUNKS
    wanted = targets.reshape(rows, CHUNKS, cc).transpose(1, 0, 2)
    xs = max(1, round(lat_size ** (1 / 3)))
    if rows % 16 == 0 and layer_size > 1 and 1 < xs < lat_size and lat_size % xs == 0:
        signal = exchange(recon, wanted, lat_size // xs, xs, layer_size, scale)
    else:
        summed = lax.psum_scatter(
            recon.astype(jnp.float32), ("lat", "layer"), scatter_dimension=1, tiled=True
        )
        mine = ((summed - wanted.astype(jnp.float32)) / scale).astype(jnp.bfloat16)
        signal = lax.all_gather(mine, ("lat", "layer"), axis=1, tiled=True)
    genc, gdec, gbias = grads(hits, act, decoder[0], signal, resid[0])
    return genc[None], gdec[None], gbias


def solution(mesh):
    placed = (
        P("layer", "grp", None),
        P(("grp", "lat", "layer"), None, None),
        P("layer", "lat", None),
        P("layer", "lat"),
        P("layer", None, "lat", None),
        P("layer", "grp", None),
    )
    return jax.shard_map(
        functools.partial(per_device, mesh.shape["lat"], mesh.shape["layer"]),
        mesh=mesh,
        in_specs=placed,
        out_specs=(
            P(("grp", "layer"), "lat", None),
            P(("grp", "layer"), None, "lat", None),
            P(("grp", "layer"), "lat"),
        ),
        check_vma=False,
    )
```

```python
import functools
import math

import jax
import jax.numpy as jnp
from jax import lax
from jax.experimental import pallas as pl
from jax.experimental.pallas import tpu as pltpu
from jax.sharding import PartitionSpec as P

BLOCK = 128
TILE = 128
CHUNKS = 8
MIB = 1 << 20
MESH = pl.DeviceIdType.MESH


def dot_nt(a, b):
    return lax.dot_general(a, b, (((1,), (1,)), ((), ())), preferred_element_type=jnp.float32)


def dot_nn(a, b):
    return jnp.dot(a, b, preferred_element_type=jnp.float32)


def chunk_place(k, width, cc):
    per = width // cc
    return k // per, (k % per) * cc


def encode_kernel(hits, resid_ref, enc_ref, bias_ref, act_ref):
    b = pl.program_id(0)
    tokens, size = act_ref.shape
    per = size // BLOCK
    pre = dot_nt(resid_ref[...], enc_ref[...]) + bias_ref[...]
    for n in range(tokens // TILE):
        for h in range(per):
            hit = hits[n, b * per + h].astype(jnp.float32)
            rows = slice(n * TILE, (n + 1) * TILE)
            cols = slice(h * BLOCK, (h + 1) * BLOCK)
            act_ref[rows, cols] = (pre[rows, cols] * hit).astype(jnp.bfloat16)


def encode(hits, resid, encoder, enc_bias):
    tokens, width = resid.shape
    latents = encoder.shape[0]
    size = min(2 * BLOCK, latents)
    return pl.pallas_call(
        encode_kernel,
        grid_spec=pltpu.PrefetchScalarGridSpec(
            num_scalar_prefetch=1,
            grid=(latents // size,),
            in_specs=[
                pl.BlockSpec((tokens, width), lambda b, h: (0, 0)),
                pl.BlockSpec((size, width), lambda b, h: (b, 0)),
                pl.BlockSpec((1, size), lambda b, h: (0, b)),
            ],
            out_specs=pl.BlockSpec((tokens, size), lambda b, h: (0, b)),
        ),
        out_shape=jax.ShapeDtypeStruct((tokens, latents), jnp.bfloat16),
        compiler_params=pltpu.CompilerParams(vmem_limit_bytes=32 * MIB),
        name="encode",
    )(hits, resid, encoder, enc_bias)


def grads_kernel(act_ref, ga_ref, sig_ref, resid_ref, genc_ref, gdec_ref):
    chunks, _, cc = sig_ref.shape
    width = resid_ref.shape[1]
    act = act_ref[...].astype(jnp.float32).T.astype(jnp.bfloat16)
    for k in range(chunks):
        t, col = chunk_place(k, width, cc)
        gdec_ref[t, :, col : col + cc] = dot_nn(act, sig_ref[k]).astype(jnp.bfloat16)
    back = ga_ref[...].astype(jnp.float32).T.astype(jnp.bfloat16)
    for col in range(0, width, cc):
        genc_ref[:, col : col + cc] = dot_nn(back, resid_ref[:, col : col + cc]).astype(jnp.bfloat16)


def grads(act, ga, signal, resid, targets):
    tokens, width = resid.shape
    latents = act.shape[1]
    chunks, _, cc = signal.shape
    size = min(2 * BLOCK, latents)
    return pl.pallas_call(
        grads_kernel,
        grid=(latents // size,),
        in_specs=[
            pl.BlockSpec((tokens, size), lambda b: (0, b)),
            pl.BlockSpec((tokens, size), lambda b: (0, b)),
            pl.BlockSpec((chunks, tokens, cc), lambda b: (0, 0, 0)),
            pl.BlockSpec((tokens, width), lambda b: (0, 0)),
        ],
        out_specs=[
            pl.BlockSpec((size, width), lambda b: (b, 0)),
            pl.BlockSpec((targets, size, width), lambda b: (0, b, 0)),
        ],
        out_shape=[
            jax.ShapeDtypeStruct((latents, width), jnp.bfloat16),
            jax.ShapeDtypeStruct((targets, latents, width), jnp.bfloat16),
        ],
        compiler_params=pltpu.CompilerParams(vmem_limit_bytes=48 * MIB),
        name="gradients",
    )(act, ga, signal, resid)


def exchange_kernel(
    scale, act_hbm, dec_hbm, tgt_ref, gate_ref, out_ref, ga_ref, bias_ref,
    p_ref, act_ref, dec_ref, acc_ref, r0, s1, r1, s2, r2,
    core_send, core_recv, x_send, x_recv, z_send, z_recv, act_sem, dec_sem,
):
    chunks, zs, xs, cores, rows, cc = p_ref.shape
    lat = lax.axis_index("lat")
    c = lax.axis_index("layer")
    z, x = lat // xs, lax.rem(lat, xs)
    f32 = jnp.float32

    def dev(dz, dx, dc):
        zz, xx = lax.rem(z + dz, zs), lax.rem(x + dx, xs)
        return {"lat": zz * xs + xx, "layer": lax.rem(c + dc, cores)}

    peers = [dev(0, 0, d) for d in range(1, cores)]
    peers += [dev(0, d, 0) for d in range(1, xs)]
    peers += [dev(d, 0, 0) for d in range(1, zs)]
    tokens, latents = act_ref.shape
    width = dec_hbm.shape[2]
    per = width // cc

    def load_dec(k):
        cols = pl.ds(pl.multiple_of(lax.rem(k, per) * cc, cc), cc)
        return pltpu.make_async_copy(dec_hbm.at[k // per, :, cols], dec_ref.at[k], dec_sem.at[k])

    load_act = pltpu.make_async_copy(act_hbm, act_ref, act_sem)
    load_act.start()
    for k in range(chunks):
        load_dec(jnp.int32(k)).start()
    barrier = pltpu.get_barrier_semaphore()
    for peer in peers:
        pl.semaphore_signal(barrier, inc=1, device_id=peer, device_id_type=MESH)
    pl.semaphore_wait(barrier, len(peers))

    def copy(src, dst, send, recv, to):
        return pltpu.make_async_remote_copy(
            src_ref=src, dst_ref=dst, send_sem=send, recv_sem=recv, device_id=to, device_id_type=MESH
        )

    def go(*a):
        copy(*a).start()

    def core_rs(k, d):
        to = lax.rem(c + d, cores)
        return (p_ref.at[k, :, :, to], r0.at[k, d - 1], core_send.at[0, k, d - 1],
                core_recv.at[0, k, d - 1], dev(0, 0, d))

    def x_rs(k, d):
        return (s1.at[k, d - 1], r1.at[k, d - 1], x_send.at[0, k, d - 1], x_recv.at[0, k, d - 1],
                dev(0, d, 0))

    def z_rs(k, d):
        return (s2.at[k, d - 1], r2.at[k, d - 1], z_send.at[0, k, d - 1], z_recv.at[0, k, d - 1],
                dev(d, 0, 0))

    def z_ag(k, d, zz):
        at = out_ref.at[k, zz, x, c]
        return (at, at, z_send.at[1, k, d - 1], z_recv.at[1, k, d - 1], dev(d, 0, 0))

    def x_ag(k, d, xx):
        at = out_ref.at[k, :, xx, c]
        return (at, at, x_send.at[1, k, d - 1], x_recv.at[1, k, d - 1], dev(0, d, 0))

    def core_ag(k, d, c2):
        at = out_ref.at[k, :, :, c2]
        return (at, at, core_send.at[1, k, d - 1], core_recv.at[1, k, d - 1], dev(0, 0, d))

    def part(k, zz, xx):
        total = p_ref[k, zz, xx, c].astype(f32)
        for i in range(cores - 1):
            total = total + r0[k, i, zz, xx].astype(f32)
        return total

    def stage_a(k):
        load_dec(k).wait()
        part_sum = dot_nn(act_ref[...], dec_ref[k]).astype(jnp.bfloat16)
        p_ref[k] = part_sum.reshape(zs, xs, cores, rows, cc)
        for d in range(1, cores):
            go(*core_rs(k, d))

    def stage_b(k):
        for d in range(1, cores):
            copy(*core_rs(k, d)).wait_recv()
        for d in range(1, xs):
            xx = lax.rem(x + d, xs)
            for zz in range(zs):
                s1[k, d - 1, zz] = part(k, zz, xx).astype(jnp.bfloat16)
            go(*x_rs(k, d))

    def line(k, zz):
        total = part(k, zz, x)
        for i in range(xs - 1):
            total = total + r1[k, i, zz].astype(f32)
        return total

    def stage_c(k):
        for d in range(1, xs):
            copy(*x_rs(k, d)).wait_recv()
        for d in range(1, zs):
            s2[k, d - 1] = line(k, lax.rem(z + d, zs)).astype(jnp.bfloat16)
            go(*z_rs(k, d))

    def stage_d(k):
        total = line(k, z)
        for d in range(1, zs):
            copy(*z_rs(k, d)).wait_recv()
            total = total + r2[k, d - 1].astype(f32)
        out_ref[k, z, x, c] = ((total - tgt_ref[k].astype(f32)) / scale).astype(jnp.bfloat16)
        for d in range(1, zs):
            go(*z_ag(k, d, z))

    def stage_e(k):
        for d in range(1, zs):
            copy(*z_ag(k, d, lax.rem(z - d + zs, zs))).wait_recv()
        for d in range(1, xs):
            go(*x_ag(k, d, x))

    def stage_f(k):
        for d in range(1, xs):
            copy(*x_ag(k, d, lax.rem(x - d + xs, xs))).wait_recv()
        for d in range(1, cores):
            go(*core_ag(k, d, c))

    def stage_g(k):
        for d in range(1, cores):
            copy(*core_ag(k, d, lax.rem(c - d + cores, cores))).wait_recv()
        sig = out_ref[k].reshape(tokens, cc)

        @pl.loop(0, latents // step)
        def _(i):
            cols = pl.ds(pl.multiple_of(i * step, step), step)
            acc_ref[:, cols] += dot_nt(sig, dec_ref[k, cols])

    step = min(512, latents)
    acc_ref[...] = jnp.zeros_like(acc_ref)
    load_act.wait()
    stages = (stage_a, stage_b, stage_c, stage_d, stage_e, stage_f, stage_g)

    @pl.loop(0, chunks + len(stages) - 1)
    def _(s):
        for i, stage in enumerate(stages):
            k = s - i

            @pl.when((k >= 0) & (k < chunks))
            def _(k=k, stage=stage):
                stage(k)

    for n in range(tokens // TILE):
        at = slice(n * TILE, (n + 1) * TILE)
        back = acc_ref[at] * gate_ref[n]
        total = jnp.sum(back, axis=0, keepdims=True)
        bias_ref[...] = total if n == 0 else bias_ref[...] + total
        ga_ref[at] = back.astype(jnp.bfloat16)

    @pl.loop(0, chunks)
    def _(k):
        for d in range(1, cores):
            copy(*core_rs(k, d)).wait_send()
            copy(*core_ag(k, d, c)).wait_send()
        for d in range(1, xs):
            copy(*x_rs(k, d)).wait_send()
            copy(*x_ag(k, d, x)).wait_send()
        for d in range(1, zs):
            copy(*z_rs(k, d)).wait_send()
            copy(*z_ag(k, d, z)).wait_send()


def exchange(act, decoder, targets, gate, chunks, zs, xs, cores, scale):
    tokens, latents = act.shape
    outs, _, width = decoder.shape
    cc = outs * width // chunks
    rows = tokens // (zs * xs * cores)
    bf16 = jnp.bfloat16
    dma = pltpu.SemaphoreType.DMA
    vmem = pl.BlockSpec(memory_space=pltpu.VMEM)
    hbm = pl.BlockSpec(memory_space=pl.ANY)
    signal, ga, bias = pl.pallas_call(
        functools.partial(exchange_kernel, scale),
        out_shape=[
            jax.ShapeDtypeStruct((chunks, zs, xs, cores, rows, cc), bf16),
            jax.ShapeDtypeStruct((tokens, latents), bf16),
            jax.ShapeDtypeStruct((1, latents), jnp.float32),
        ],
        in_specs=[hbm, hbm, vmem, vmem],
        out_specs=[vmem, vmem, vmem],
        scratch_shapes=[
            pltpu.VMEM((chunks, zs, xs, cores, rows, cc), bf16),
            pltpu.VMEM((tokens, latents), bf16),
            pltpu.VMEM((chunks, latents, cc), bf16),
            pltpu.VMEM((tokens, latents), jnp.float32),
            pltpu.VMEM((chunks, cores - 1, zs, xs, rows, cc), bf16),
            pltpu.VMEM((chunks, xs - 1, zs, rows, cc), bf16),
            pltpu.VMEM((chunks, xs - 1, zs, rows, cc), bf16),
            pltpu.VMEM((chunks, zs - 1, rows, cc), bf16),
            pltpu.VMEM((chunks, zs - 1, rows, cc), bf16),
            dma((2, chunks, cores - 1)),
            dma((2, chunks, cores - 1)),
            dma((2, chunks, xs - 1)),
            dma((2, chunks, xs - 1)),
            dma((2, chunks, zs - 1)),
            dma((2, chunks, zs - 1)),
            dma,
            dma((chunks,)),
        ],
        compiler_params=pltpu.CompilerParams(
            collective_id=0, has_side_effects=True, vmem_limit_bytes=56 * MIB
        ),
        name="exchange",
    )(act, decoder, targets, gate)
    return signal.reshape(chunks, tokens, cc), ga, bias


def per_device(lat_size, layer_size, resid, targets, encoder, enc_bias, decoder, blocks):
    lat_count = encoder.shape[1]
    width = resid.shape[2]
    tokens = resid.shape[1]
    outs = decoder.shape[1]
    nb = lat_count // BLOCK
    lat_block = lax.axis_index("lat") * nb + jnp.arange(nb, dtype=jnp.int32)
    hits = jnp.any(blocks[0][:, :, None] == lat_block[None, None, :], axis=1).astype(jnp.int32)
    scale = math.sqrt(tokens)
    gate = jnp.repeat(hits, BLOCK, axis=1).astype(jnp.float32)[:, None, :]
    act = encode(hits, resid[0], encoder[0], enc_bias)
    rows = targets.shape[0]
    cc = outs * width // CHUNKS
    wanted = targets.reshape(rows, CHUNKS, cc).transpose(1, 0, 2)
    xs = max(1, round(lat_size ** (1 / 3)))
    if rows % 16 == 0 and layer_size > 1 and 1 < xs < lat_size and lat_size % xs == 0:
        signal, ga, gbias = exchange(
            act, decoder[0], wanted, gate, CHUNKS, lat_size // xs, xs, layer_size, scale
        )
    else:
        f32 = jnp.float32
        by_chunk = decoder[0].reshape(outs, lat_count, CHUNKS // outs, cc)
        by_chunk = by_chunk.transpose(0, 2, 1, 3).reshape(CHUNKS, lat_count, cc)
        recon = jnp.einsum("nl,kld->knd", act, by_chunk, preferred_element_type=f32)
        summed = lax.psum_scatter(recon, ("lat", "layer"), scatter_dimension=1, tiled=True)
        mine = ((summed - wanted.astype(f32)) / scale).astype(jnp.bfloat16)
        signal = lax.all_gather(mine, ("lat", "layer"), axis=1, tiled=True)
        back = jnp.einsum("knd,kld->nl", signal, by_chunk, preferred_element_type=f32)
        back = back * jnp.repeat(gate[:, 0], TILE, axis=0)
        gbias = jnp.sum(back, axis=0, keepdims=True)
        ga = back.astype(jnp.bfloat16)
    genc, gdec = grads(act, ga, signal, resid[0], outs)
    return genc[None], gdec[None], gbias


def solution(mesh):
    placed = (
        P("layer", "grp", None),
        P(("grp", "lat", "layer"), None, None),
        P("layer", "lat", None),
        P("layer", "lat"),
        P("layer", None, "lat", None),
        P("layer", "grp", None),
    )
    return jax.shard_map(
        functools.partial(per_device, mesh.shape["lat"], mesh.shape["layer"]),
        mesh=mesh,
        in_specs=placed,
        out_specs=(
            P(("grp", "layer"), "lat", None),
            P(("grp", "layer"), None, "lat", None),
            P(("grp", "layer"), "lat"),
        ),
        check_vma=False,
    )
```

```python
import functools
import math

import jax
import jax.numpy as jnp
from jax import lax
from jax.experimental import pallas as pl
from jax.experimental.pallas import tpu as pltpu
from jax.sharding import PartitionSpec as P

BLOCK = 128
TILE = 128
CHUNKS = 8
MIB = 1 << 20
MESH = pl.DeviceIdType.MESH


def dot_nt(a, b):
    return lax.dot_general(a, b, (((1,), (1,)), ((), ())), preferred_element_type=jnp.float32)


def dot_nn(a, b):
    return jnp.dot(a, b, preferred_element_type=jnp.float32)


def chunk_place(k, width, cc):
    per = width // cc
    return k // per, (k % per) * cc


def encode_kernel(hits, resid_ref, enc_ref, bias_ref, act_ref):
    b = pl.program_id(0)
    tokens, size = act_ref.shape
    per = size // BLOCK
    pre = dot_nt(resid_ref[...], enc_ref[...]) + bias_ref[...]
    for n in range(tokens // TILE):
        for h in range(per):
            hit = hits[n, b * per + h].astype(jnp.float32)
            rows = slice(n * TILE, (n + 1) * TILE)
            cols = slice(h * BLOCK, (h + 1) * BLOCK)
            act_ref[rows, cols] = (pre[rows, cols] * hit).astype(jnp.bfloat16)


def encode(hits, resid, encoder, enc_bias):
    tokens, width = resid.shape
    latents = encoder.shape[0]
    size = min(2 * BLOCK, latents)
    return pl.pallas_call(
        encode_kernel,
        grid_spec=pltpu.PrefetchScalarGridSpec(
            num_scalar_prefetch=1,
            grid=(latents // size,),
            in_specs=[
                pl.BlockSpec((tokens, width), lambda b, h: (0, 0)),
                pl.BlockSpec((size, width), lambda b, h: (b, 0)),
                pl.BlockSpec((1, size), lambda b, h: (0, b)),
            ],
            out_specs=pl.BlockSpec((tokens, size), lambda b, h: (0, b)),
        ),
        out_shape=jax.ShapeDtypeStruct((tokens, latents), jnp.bfloat16),
        compiler_params=pltpu.CompilerParams(vmem_limit_bytes=60 * MIB),
        name="encode",
    )(hits, resid, encoder, enc_bias)


def grads_kernel(act_ref, ga_ref, sig_ref, resid_ref, genc_ref, gdec_ref):
    chunks, _, cc = sig_ref.shape
    width = resid_ref.shape[1]
    act = act_ref[...].astype(jnp.float32).T.astype(jnp.bfloat16)
    for k in range(chunks):
        t, col = chunk_place(k, width, cc)
        gdec_ref[t, :, col : col + cc] = dot_nn(act, sig_ref[k]).astype(jnp.bfloat16)
    back = ga_ref[...].astype(jnp.float32).T.astype(jnp.bfloat16)
    for col in range(0, width, cc):
        genc_ref[:, col : col + cc] = dot_nn(back, resid_ref[:, col : col + cc]).astype(jnp.bfloat16)


def grads(act, ga, signal, resid, targets):
    tokens, width = resid.shape
    latents = act.shape[1]
    chunks, _, cc = signal.shape
    size = min(2 * BLOCK, latents)
    return pl.pallas_call(
        grads_kernel,
        grid=(latents // size,),
        in_specs=[
            pl.BlockSpec((tokens, size), lambda b: (0, b)),
            pl.BlockSpec((tokens, size), lambda b: (0, b)),
            pl.BlockSpec((chunks, tokens, cc), lambda b: (0, 0, 0)),
            pl.BlockSpec((tokens, width), lambda b: (0, 0)),
        ],
        out_specs=[
            pl.BlockSpec((size, width), lambda b: (b, 0)),
            pl.BlockSpec((targets, size, width), lambda b: (0, b, 0)),
        ],
        out_shape=[
            jax.ShapeDtypeStruct((latents, width), jnp.bfloat16),
            jax.ShapeDtypeStruct((targets, latents, width), jnp.bfloat16),
        ],
        compiler_params=pltpu.CompilerParams(vmem_limit_bytes=60 * MIB),
        name="gradients",
    )(act, ga, signal, resid)


def exchange_kernel(
    scale, act_hbm, dec_hbm, tgt_ref, gate_ref, out_ref, ga_ref, bias_ref,
    p_ref, act_ref, dec_ref, acc_ref, r0, s1, r1, s2, r2,
    core_send, core_recv, x_send, x_recv, z_send, z_recv, act_sem, dec_sem,
):
    chunks, zs, xs, cores, rows, cc = p_ref.shape
    lat = lax.axis_index("lat")
    c = lax.axis_index("layer")
    z, x = lat // xs, lax.rem(lat, xs)
    f32 = jnp.float32

    def dev(dz, dx, dc):
        zz, xx = lax.rem(z + dz, zs), lax.rem(x + dx, xs)
        return {"lat": zz * xs + xx, "layer": lax.rem(c + dc, cores)}

    peers = [dev(0, 0, d) for d in range(1, cores)]
    peers += [dev(0, d, 0) for d in range(1, xs)]
    peers += [dev(d, 0, 0) for d in range(1, zs)]
    tokens, latents = act_ref.shape
    width = dec_hbm.shape[2]
    per = width // cc

    def load_dec(k):
        cols = pl.ds(pl.multiple_of(lax.rem(k, per) * cc, cc), cc)
        return pltpu.make_async_copy(dec_hbm.at[k // per, :, cols], dec_ref.at[k], dec_sem.at[k])

    load_act = pltpu.make_async_copy(act_hbm, act_ref, act_sem)
    load_act.start()
    for k in range(chunks):
        load_dec(jnp.int32(k)).start()
    barrier = pltpu.get_barrier_semaphore()
    for peer in peers:
        pl.semaphore_signal(barrier, inc=1, device_id=peer, device_id_type=MESH)
    pl.semaphore_wait(barrier, len(peers))

    def copy(src, dst, send, recv, to):
        return pltpu.make_async_remote_copy(
            src_ref=src, dst_ref=dst, send_sem=send, recv_sem=recv, device_id=to, device_id_type=MESH
        )

    def go(*a):
        copy(*a).start()

    def core_rs(k, d):
        to = lax.rem(c + d, cores)
        return (p_ref.at[k, :, :, to], r0.at[k, d - 1], core_send.at[0, k, d - 1],
                core_recv.at[0, k, d - 1], dev(0, 0, d))

    def x_rs(k, d):
        return (s1.at[k, d - 1], r1.at[k, d - 1], x_send.at[0, k, d - 1], x_recv.at[0, k, d - 1],
                dev(0, d, 0))

    def z_rs(k, d):
        return (s2.at[k, d - 1], r2.at[k, d - 1], z_send.at[0, k, d - 1], z_recv.at[0, k, d - 1],
                dev(d, 0, 0))

    def z_ag(k, d, zz):
        at = out_ref.at[k, zz, x, c]
        return (at, at, z_send.at[1, k, d - 1], z_recv.at[1, k, d - 1], dev(d, 0, 0))

    def x_ag(k, d, xx):
        at = out_ref.at[k, :, xx, c]
        return (at, at, x_send.at[1, k, d - 1], x_recv.at[1, k, d - 1], dev(0, d, 0))

    def core_ag(k, d, c2):
        at = out_ref.at[k, :, :, c2]
        return (at, at, core_send.at[1, k, d - 1], core_recv.at[1, k, d - 1], dev(0, 0, d))

    def part(k, zz, xx):
        total = p_ref[k, zz, xx, c].astype(f32)
        for i in range(cores - 1):
            total = total + r0[k, i, zz, xx].astype(f32)
        return total

    def stage_a(k):
        load_dec(k).wait()
        part_sum = dot_nn(act_ref[...], dec_ref[k]).astype(jnp.bfloat16)
        p_ref[k] = part_sum.reshape(zs, xs, cores, rows, cc)
        for d in range(1, cores):
            go(*core_rs(k, d))

    def stage_b(k):
        for d in range(1, cores):
            copy(*core_rs(k, d)).wait_recv()
        for d in range(1, xs):
            xx = lax.rem(x + d, xs)
            for zz in range(zs):
                s1[k, d - 1, zz] = part(k, zz, xx).astype(jnp.bfloat16)
            go(*x_rs(k, d))

    def line(k, zz):
        total = part(k, zz, x)
        for i in range(xs - 1):
            total = total + r1[k, i, zz].astype(f32)
        return total

    def stage_c(k):
        for d in range(1, xs):
            copy(*x_rs(k, d)).wait_recv()
        for d in range(1, zs):
            s2[k, d - 1] = line(k, lax.rem(z + d, zs)).astype(jnp.bfloat16)
            go(*z_rs(k, d))

    def stage_d(k):
        total = line(k, z)
        for d in range(1, zs):
            copy(*z_rs(k, d)).wait_recv()
            total = total + r2[k, d - 1].astype(f32)
        out_ref[k, z, x, c] = ((total - tgt_ref[k].astype(f32)) / scale).astype(jnp.bfloat16)
        for d in range(1, zs):
            go(*z_ag(k, d, z))

    def stage_e(k):
        for d in range(1, zs):
            copy(*z_ag(k, d, lax.rem(z - d + zs, zs))).wait_recv()
        for d in range(1, xs):
            go(*x_ag(k, d, x))

    def stage_f(k):
        for d in range(1, xs):
            copy(*x_ag(k, d, lax.rem(x - d + xs, xs))).wait_recv()
        for d in range(1, cores):
            go(*core_ag(k, d, c))

    def stage_g(k):
        for d in range(1, cores):
            copy(*core_ag(k, d, lax.rem(c - d + cores, cores))).wait_recv()
        sig = out_ref[k].reshape(tokens, cc)

        @pl.loop(0, latents // step)
        def _(i):
            cols = pl.ds(pl.multiple_of(i * step, step), step)
            acc_ref[:, cols] += dot_nt(sig, dec_ref[k, cols])

    step = min(512, latents)
    acc_ref[...] = jnp.zeros_like(acc_ref)
    load_act.wait()
    stages = (stage_a, stage_b, stage_c, stage_d, stage_e, stage_f, stage_g)

    @pl.loop(0, chunks + len(stages) - 1)
    def _(s):
        for i, stage in enumerate(stages):
            k = s - i

            @pl.when((k >= 0) & (k < chunks))
            def _(k=k, stage=stage):
                stage(k)

    for n in range(tokens // TILE):
        at = slice(n * TILE, (n + 1) * TILE)
        back = acc_ref[at] * gate_ref[n]
        total = jnp.sum(back, axis=0, keepdims=True)
        bias_ref[...] = total if n == 0 else bias_ref[...] + total
        ga_ref[at] = back.astype(jnp.bfloat16)

    @pl.loop(0, chunks)
    def _(k):
        for d in range(1, cores):
            copy(*core_rs(k, d)).wait_send()
            copy(*core_ag(k, d, c)).wait_send()
        for d in range(1, xs):
            copy(*x_rs(k, d)).wait_send()
            copy(*x_ag(k, d, x)).wait_send()
        for d in range(1, zs):
            copy(*z_rs(k, d)).wait_send()
            copy(*z_ag(k, d, z)).wait_send()


def exchange(act, decoder, targets, gate, chunks, zs, xs, cores, scale):
    tokens, latents = act.shape
    outs, _, width = decoder.shape
    cc = outs * width // chunks
    rows = tokens // (zs * xs * cores)
    bf16 = jnp.bfloat16
    dma = pltpu.SemaphoreType.DMA
    vmem = pl.BlockSpec(memory_space=pltpu.VMEM)
    hbm = pl.BlockSpec(memory_space=pl.ANY)
    signal, ga, bias = pl.pallas_call(
        functools.partial(exchange_kernel, scale),
        out_shape=[
            jax.ShapeDtypeStruct((chunks, zs, xs, cores, rows, cc), bf16),
            jax.ShapeDtypeStruct((tokens, latents), bf16),
            jax.ShapeDtypeStruct((1, latents), jnp.float32),
        ],
        in_specs=[hbm, hbm, vmem, vmem],
        out_specs=[vmem, vmem, vmem],
        scratch_shapes=[
            pltpu.VMEM((chunks, zs, xs, cores, rows, cc), bf16),
            pltpu.VMEM((tokens, latents), bf16),
            pltpu.VMEM((chunks, latents, cc), bf16),
            pltpu.VMEM((tokens, latents), jnp.float32),
            pltpu.VMEM((chunks, cores - 1, zs, xs, rows, cc), bf16),
            pltpu.VMEM((chunks, xs - 1, zs, rows, cc), bf16),
            pltpu.VMEM((chunks, xs - 1, zs, rows, cc), bf16),
            pltpu.VMEM((chunks, zs - 1, rows, cc), bf16),
            pltpu.VMEM((chunks, zs - 1, rows, cc), bf16),
            dma((2, chunks, cores - 1)),
            dma((2, chunks, cores - 1)),
            dma((2, chunks, xs - 1)),
            dma((2, chunks, xs - 1)),
            dma((2, chunks, zs - 1)),
            dma((2, chunks, zs - 1)),
            dma,
            dma((chunks,)),
        ],
        compiler_params=pltpu.CompilerParams(
            collective_id=0, has_side_effects=True, vmem_limit_bytes=60 * MIB
        ),
        name="exchange",
    )(act, decoder, targets, gate)
    return signal.reshape(chunks, tokens, cc), ga, bias


def per_device(lat_size, layer_size, resid, targets, encoder, enc_bias, decoder, blocks):
    lat_count = encoder.shape[1]
    width = resid.shape[2]
    tokens = resid.shape[1]
    outs = decoder.shape[1]
    nb = lat_count // BLOCK
    lat_block = lax.axis_index("lat") * nb + jnp.arange(nb, dtype=jnp.int32)
    hits = jnp.any(blocks[0][:, :, None] == lat_block[None, None, :], axis=1).astype(jnp.int32)
    scale = math.sqrt(tokens)
    gate = jnp.repeat(hits, BLOCK, axis=1).astype(jnp.float32)[:, None, :]
    act = encode(hits, resid[0], encoder[0], enc_bias)
    rows = targets.shape[0]
    cc = outs * width // CHUNKS
    wanted = targets.reshape(rows, CHUNKS, cc).transpose(1, 0, 2)
    xs = max(1, round(lat_size ** (1 / 3)))
    if rows % 16 == 0 and layer_size > 1 and 1 < xs < lat_size and lat_size % xs == 0:
        signal, ga, gbias = exchange(
            act, decoder[0], wanted, gate, CHUNKS, lat_size // xs, xs, layer_size, scale
        )
    else:
        f32 = jnp.float32
        by_chunk = decoder[0].reshape(outs, lat_count, CHUNKS // outs, cc)
        by_chunk = by_chunk.transpose(0, 2, 1, 3).reshape(CHUNKS, lat_count, cc)
        recon = jnp.einsum("nl,kld->knd", act, by_chunk, preferred_element_type=f32)
        summed = lax.psum_scatter(recon, ("lat", "layer"), scatter_dimension=1, tiled=True)
        mine = ((summed - wanted.astype(f32)) / scale).astype(jnp.bfloat16)
        signal = lax.all_gather(mine, ("lat", "layer"), axis=1, tiled=True)
        back = jnp.einsum("knd,kld->nl", signal, by_chunk, preferred_element_type=f32)
        back = back * jnp.repeat(gate[:, 0], TILE, axis=0)
        gbias = jnp.sum(back, axis=0, keepdims=True)
        ga = back.astype(jnp.bfloat16)
    genc, gdec = grads(act, ga, signal, resid[0], outs)
    return genc[None], gdec[None], gbias


def solution(mesh):
    placed = (
        P("layer", "grp", None),
        P(("grp", "lat", "layer"), None, None),
        P("layer", "lat", None),
        P("layer", "lat"),
        P("layer", None, "lat", None),
        P("layer", "grp", None),
    )
    return jax.shard_map(
        functools.partial(per_device, mesh.shape["lat"], mesh.shape["layer"]),
        mesh=mesh,
        in_specs=placed,
        out_specs=(
            P(("grp", "layer"), "lat", None),
            P(("grp", "layer"), None, "lat", None),
            P(("grp", "layer"), "lat"),
        ),
        check_vma=False,
    )
```
